32 devices in a mesh: pair: 16 (over z, x, core), aux: 2 (over y).
Axes of the slice: x: 2, y: 2, z: 4, core: 2. Of those that a mesh axis runs over, the one named last changes fastest.
Arguments:
- doubles: bfloat16 [32, 512, 512], P('pair', 'aux'), may hold values from -1.796875 to 1.796875
- singles: bfloat16 [256, 512], replicated, may hold values from -0.8984375 to 0.8984375
- vir_slabs: bfloat16 [4096, 8, 512], P(('aux', 'pair')), may hold values from -0.059814453 to 0.059814453
- occ_slabs: bfloat16 [4096, 256, 512], P(('aux', 'pair')), may hold values from -0.029907227 to 0.029907227
- occ_energy: float32 [256], replicated, may hold values from -2 to -0.5
- vir_energy: float32 [8], replicated, may hold values from 0.1 to 1.5
- pair_list: int32 [32, 2], P('pair'), may hold values from 0 to 255
Outputs:
- new_doubles: float32 [32, 8, 8], P('pair', 'aux')
The draws below stay inside these ranges and needn't reach their ends.
All inputs are finite; a program needn't handle non-finite values.
Results may differ from the reference program's by a relative error of at most 0.0005.
Values may be sent and summed in bfloat16 or wider, within the bound.
A program may use at most 128 MiB of HBM per device.

```python
import jax
import jax.numpy as jnp
from jax import lax

V = 512
O = 256
NAUX = 4096
NWIN = 8
PAIRS = 32


def set_ends(values, key, least, largest):
    longest = values.shape.index(max(values.shape))
    spots = []
    for shift in (0, 1):
        where = [jax.random.randint(jax.random.fold_in(key, axis), (), 0, length) for axis, length in enumerate(values.shape)]
        where[longest] = (where[longest] + shift) % values.shape[longest]
        spots.append(tuple(where))
    return values.at[spots[0]].set(least).at[spots[1]].set(largest)


def block_scale(rng, dims, shards, least, high):
    def one(axis_at, parts):
        draws = jax.random.uniform(jax.random.fold_in(jax.random.fold_in(rng, 6), axis_at), (parts,), jnp.float32, least / len(shards), high / len(shards))
        return jnp.repeat(jnp.exp(draws), dims[axis_at] // parts).reshape((-1,) + (1,) * (len(dims) - axis_at - 1))

    factor_of = one(*shards[0])
    for cut in shards[1:]:
        factor_of = factor_of * one(*cut)
    return factor_of


def normal_values(rng, dims, spread, limit, cuts=(), held_as=jnp.bfloat16):
    values = spread * jax.random.normal(rng, dims, jnp.float32)
    if cuts:
        values = values * block_scale(rng, dims, cuts, -0.22, 0.18)
    return jnp.clip(values, -limit, limit).astype(held_as)


def setup_inputs(seed: int = 0) -> dict:
    splits = jax.random.split(jax.random.key(seed), 8)
    doubles = normal_values(splits[0], (PAIRS, V, V), 0.3, 1.796875, ((0, 16), (1, 2)))
    singles = normal_values(splits[1], (O, V), 0.15, 0.8984375)
    vir_slabs = normal_values(splits[2], (NAUX, NWIN, V), 0.01, 0.059814453, ((0, 32),))
    occ_slabs = normal_values(splits[3], (NAUX, O, V), 0.005, 0.029907227, ((0, 32),))
    occ_energy = jnp.clip(jax.random.uniform(splits[4], (O,), jnp.float32, -2.0, -0.5), -2.0, -0.5)
    vir_energy = jnp.clip(jax.random.uniform(splits[5], (NWIN,), jnp.float32, 0.1, 1.5), 0.1, 1.5)
    pair_list = set_ends(jax.random.randint(splits[6], (PAIRS, 2), 0, O), jax.random.fold_in(splits[6], 1), 0, O - 1).astype(jnp.int32)
    return {"doubles": doubles, "singles": singles, "vir_slabs": vir_slabs, "occ_slabs": occ_slabs, "occ_energy": occ_energy, "vir_energy": vir_energy, "pair_list": pair_list}


def reference(doubles, singles, vir_slabs, occ_slabs, occ_energy, vir_energy, pair_list):
    first_occ = pair_list[:, 0]
    second_occ = pair_list[:, 1]
    row_first = singles[first_occ].astype(jnp.float32)
    row_second = singles[second_occ].astype(jnp.float32)
    tau_amps = (doubles.astype(jnp.float32) + row_first[:, :, None] * row_second[:, None, :]).astype(jnp.bfloat16)
    tau_wide = tau_amps.astype(jnp.float32)
    dressing_cols = singles[:, :NWIN].astype(jnp.float32)
    block_size = 64 if NAUX % 64 == 0 else NAUX
    block_count = NAUX // block_size
    vir_blocks = vir_slabs.reshape(block_count, block_size, NWIN, V)
    occ_blocks = occ_slabs.reshape(block_count, block_size, O, V)

    def accumulate(running, blocks):
        vir_part, occ_part = blocks
        dressed = (vir_part.astype(jnp.float32) - jnp.einsum('ka,qkc->qac', dressing_cols, occ_part.astype(jnp.float32))).astype(jnp.bfloat16)
        dressed_wide = dressed.astype(jnp.float32)
        half_done = jnp.einsum('qac,pcd->pqad', dressed_wide, tau_wide).astype(jnp.bfloat16)
        running = running + jnp.einsum('pqad,qbd->pab', half_done.astype(jnp.float32), dressed_wide)
        return running, None

    residual, _ = lax.scan(accumulate, jnp.zeros((PAIRS, NWIN, NWIN), jnp.float32), (vir_blocks, occ_blocks))
    pair_energy = occ_energy[first_occ] + occ_energy[second_occ]
    denominator = pair_energy[:, None, None] - vir_energy[None, :, None] - vir_energy[None, None, :]
    return doubles[:, :NWIN, :NWIN].astype(jnp.float32) + residual / denominator
```

```python
import functools
import math

import jax
import jax.numpy as jnp
from jax import lax
from jax.experimental import pallas as pl
from jax.experimental.pallas import tpu as pltpu
from jax.sharding import PartitionSpec as P

MESH = pl.DeviceIdType.MESH


def inner_group(n_pair):
    size = 2
    while size * size < n_pair:
        size *= 2
    return math.gcd(size, n_pair)


def ladder_kernel(
    n_pair, n_aux, group, win,
    tau_ref, lhs_ref, vir_ref, tile_ref, occ_ref,
    out_ref, tile_out_ref,
    tau, dressed, slabs, half_buf, total, fold, parts, tiles,
    own_sem, slab_sem, z_send, z_recv, y_send, y_recv,
    x_send, x_recv, c_send, c_recv, r_send, r_recv, t_send, t_recv,
):
    lines = n_pair // group
    cols = group // 2
    per_dev, rows_c, width = tau_ref.shape
    rows = vir_ref.shape[0]
    sends = x_recv.shape[1]
    send_rows = rows // sends
    slab_rows = slabs.shape[1]
    depth = lhs_ref.shape[1]
    steps = occ_ref.shape[0] // slab_rows
    step_rows = rows // steps
    block = total.shape[1]

    pair = lax.axis_index("pair")
    aux = lax.axis_index("aux")
    z = pair // group
    g = pair % group
    col = g // 2
    core = g % 2

    def at(zz, gg, aa):
        return {"pair": zz * group + gg, "aux": aa}

    def slab_copy(step):
        slot = lax.rem(step, slabs.shape[0])
        return pltpu.make_async_copy(
            occ_ref.at[pl.ds(step * slab_rows, slab_rows)], slabs.at[slot], slab_sem.at[slot]
        )

    depth_slots = slabs.shape[0]
    for step in range(min(depth_slots, steps)):
        slab_copy(step).start()
    own_rows = pl.ds(pl.multiple_of(aux * rows_c, rows_c), rows_c)
    own = pltpu.make_async_copy(tau_ref, tau.at[z, :, own_rows], own_sem)
    own.start()
    tiles[aux] = tile_ref[...]

    barrier = pltpu.get_barrier_semaphore()
    for dz in range(lines):
        for da in range(n_aux):
            if dz or da:
                pl.semaphore_signal(
                    barrier, inc=1, device_id=at((z + dz) % lines, g, (aux + da) % n_aux), device_id_type=MESH
                )
    for dg in range(1, group):
        pl.semaphore_signal(barrier, inc=1, device_id=at(z, (g + dg) % group, aux), device_id_type=MESH)
    pl.semaphore_wait(barrier, lines * n_aux - 1 + group - 1)
    own.wait()

    def piece(zz, k, aa):
        return tau.at[zz, k, pl.ds(pl.multiple_of(aa * rows_c, rows_c), rows_c)]

    def z_copy(zz, k, way):
        ref = piece(zz, k, aux)
        return pltpu.make_async_remote_copy(
            src_ref=ref, dst_ref=ref, send_sem=z_send.at[(way + 1) // 2, zz, k],
            recv_sem=z_recv.at[zz, k], device_id=at(z + way, g, aux), device_id_type=MESH,
        )

    def y_copy(zz, k, aa, other):
        ref = piece(zz, k, aa)
        return pltpu.make_async_remote_copy(
            src_ref=ref, dst_ref=ref, send_sem=y_send.at[zz, k, other],
            recv_sem=y_recv.at[zz, k, aa], device_id=at(z, g, other), device_id_type=MESH,
        )

    def onward(zz, k, ways):
        for way in ways:
            @pl.when((z + way >= 0) & (z + way < lines))
            def _():
                z_copy(zz, k, way).start()
        for da in range(1, n_aux):
            y_copy(zz, k, aux, (aux + da) % n_aux).start()

    def relay(dist, k):
        for way in (-1, 1):
            source = z - way * dist

            @pl.when((source >= 0) & (source < lines))
            def _():
                z_copy(source, k, way).wait_recv()
                onward(source, k, (way,))

    def x_copy(owner_col, part, to_col):
        ref = dressed.at[owner_col * 2 + core, pl.ds(part * send_rows, send_rows)]
        return pltpu.make_async_remote_copy(
            src_ref=ref, dst_ref=ref, send_sem=x_send.at[to_col, part],
            recv_sem=x_recv.at[owner_col, part], device_id=at(z, to_col * 2 + core, aux), device_id_type=MESH,
        )

    def c_copy(owner_col, owner_core, part):
        ref = dressed.at[owner_col * 2 + owner_core, pl.ds(part * send_rows, send_rows)]
        return pltpu.make_async_remote_copy(
            src_ref=ref, dst_ref=ref, send_sem=c_send.at[owner_col, part],
            recv_sem=c_recv.at[owner_col, part], device_id=at(z, col * 2 + 1 - core, aux), device_id_type=MESH,
        )

    def tile_copy(source, other):
        return pltpu.make_async_remote_copy(
            src_ref=tiles.at[source], dst_ref=tiles.at[source], send_sem=t_send.at[other],
            recv_sem=t_recv.at[source], device_id=at(z, g, other), device_id_type=MESH,
        )

    def other_cols():
        return [(col + dc) % cols for dc in range(1, cols)]

    def pass_block(part):
        for owner in other_cols():
            x_copy(owner, part, owner).wait_recv()
            c_copy(owner, core, part).start()

    for k in range(per_dev):
        onward(z, k, (-1, 1))
    for da in range(1, n_aux):
        tile_copy(aux, (aux + da) % n_aux).start()

    def dress(step, carry):
        slab_copy(step).wait()
        slot = lax.rem(step, depth_slots)
        for i in range(slab_rows // depth):
            acc = jnp.dot(
                lhs_ref[...], slabs[slot, i * depth:(i + 1) * depth, :], preferred_element_type=jnp.float32
            )
            start = pl.multiple_of(step * step_rows + i * 2 * win, 2 * win)
            made = vir_ref[pl.ds(start, 2 * win), :].astype(jnp.float32) - acc
            dressed[g, pl.ds(start, 2 * win), :] = made.astype(jnp.bfloat16)

        @pl.when(step + depth_slots < steps)
        def _():
            slab_copy(step + depth_slots).start()
        return carry

    events = {}
    if lines > 1:
        for k in range(per_dev):
            when = min(steps, max(1, (steps * (7 + 5 * k)) // 16))
            events.setdefault(when, []).append(functools.partial(relay, 1, k))
    passed = 0
    for part in range(sends):
        made_at = (part + 1) * steps // sends

        def send_own(part=part):
            for to_col in other_cols():
                x_copy(col, part, to_col).start()
            c_copy(col, core, part).start()

        events.setdefault(made_at, []).append(send_own)
        if part * 2 < sends:
            later = (part + 1) * steps // sends + (6 * steps) // 16
            if later < steps:
                events.setdefault(later, []).append(functools.partial(pass_block, part))
                passed = part + 1
    begin = 0
    for stop in sorted(events):
        if stop > begin:
            lax.fori_loop(begin, stop, dress, 0)
            begin = stop
        for action in events[stop]:
            action()
    if begin < steps:
        lax.fori_loop(begin, steps, dress, 0)

    total[...] = jnp.zeros_like(total)

    def unit(zz, k, gg):
        half_buf[...] = jnp.dot(
            dressed[gg], tau[zz, k], preferred_element_type=jnp.float32
        ).astype(jnp.bfloat16)
        acc = None
        for i in range(rows // block):
            term = lax.dot_general(
                half_buf[i * block:(i + 1) * block, :],
                dressed[gg, pl.ds(i * block, block), :],
                (((1,), (1,)), ((), ())), preferred_element_type=jnp.float32,
            )
            acc = term if acc is None else acc + term
        total[zz * per_dev + k] += acc

    def nth_group(i):
        return ((col + i // 2) % cols) * 2 + (core + i % 2) % 2

    def units(zz, k, first, last):
        def one(i, carry):
            unit(zz, k, nth_group(i))
            return carry

        lax.fori_loop(first, last, one, 0)

    def nth_line(t):
        near = jnp.minimum(z, lines - 1 - z)
        side = (t + 1) // 2 * (1 - 2 * (t % 2))
        rest = jnp.where(z + z <= lines - 1, t, lines - 1 - t)
        return jnp.where(t <= 2 * near, z + side, rest)

    def arrived(zz, k):
        for da in range(1, n_aux):
            source = (aux + da) % n_aux
            y_copy(zz, k, source, source).wait_recv()

    for k in range(per_dev):
        if lines > 2:
            relay(2, k)
        arrived(z, k)
        units(z, k, 0, 1)
        if k == 0:
            for part in range(sends):
                c_copy(col, 1 - core, part).wait_recv()
        units(z, k, 1, 2)
        for part in range(passed, min(sends, passed + 1)):
            pass_block(part)
            passed = part + 1
    for part in range(passed, sends):
        pass_block(part)
    for owner in other_cols():
        for part in range(sends):
            c_copy(owner, 1 - core, part).wait_recv()
    for k in range(per_dev):
        if lines > 3:
            relay(3, k)
        units(z, k, 2, group)
    for t in range(1, lines):
        zz = nth_line(t)
        for k in range(per_dev):
            if t + 3 < lines:
                relay(t + 3, k)
            arrived(zz, k)
            units(zz, k, 0, group)

    down = lax.broadcasted_iota(jnp.int32, (block, block), 0) // win
    across = lax.broadcasted_iota(jnp.int32, (block, block), 1) // win
    on_diagonal = down == across
    for zz in range(lines):
        for k in range(per_dev):
            kept = jnp.where(on_diagonal, total[zz * per_dev + k], 0.0)
            fold[zz, k] = jnp.sum(kept.reshape(block // win, win, block), axis=0)

    def sum_copy(source_z, source_aux, to_z, to_aux):
        return pltpu.make_async_remote_copy(
            src_ref=fold.at[to_z], dst_ref=parts.at[source_z, source_aux],
            send_sem=r_send.at[to_z, to_aux], recv_sem=r_recv.at[source_z, source_aux],
            device_id=at(to_z, g, to_aux), device_id_type=MESH,
        )

    others = [
        ((z + dz) % lines, (aux + da) % n_aux)
        for dz in range(lines) for da in range(n_aux) if dz or da
    ]
    for to_z, to_aux in others:
        sum_copy(z, aux, to_z, to_aux).start()
    parts[z, aux] = fold[z]
    for from_z, from_aux in others:
        sum_copy(from_z, from_aux, from_z, from_aux).wait_recv()
    result = parts[0, 0]
    for i in range(1, lines * n_aux):
        result = result + parts[i // n_aux, i % n_aux]
    out_ref[...] = result
    for da in range(1, n_aux):
        source = (aux + da) % n_aux
        tile_copy(source, source).wait_recv()
    tile_out_ref[...] = tiles[0]

    for to_z, to_aux in others:
        sum_copy(z, aux, to_z, to_aux).wait_send()
    for da in range(1, n_aux):
        tile_copy(aux, (aux + da) % n_aux).wait_send()
    for part in range(sends):
        for to_col in other_cols():
            x_copy(col, part, to_col).wait_send()
        for dc in range(cols):
            c_copy((col + dc) % cols, core, part).wait_send()
    for k in range(per_dev):
        for zz in range(lines):
            for da in range(1, n_aux):
                y_copy(zz, k, aux, (aux + da) % n_aux).wait_send()

            @pl.when((zz <= z) & (z + 1 < lines))
            def _():
                z_copy(zz, k, 1).wait_send()

            @pl.when((zz >= z) & (z >= 1))
            def _():
                z_copy(zz, k, -1).wait_send()


def body(n_pair, n_aux, doubles, singles, vir_slabs, occ_slabs, occ_energy, vir_energy, pair_list):
    per_dev, rows_c, width = doubles.shape
    aux_count, win, _ = vir_slabs.shape
    occ_count = singles.shape[0]
    group = inner_group(n_pair)
    lines = n_pair // group
    cols = group // 2
    aux = lax.axis_index("aux")

    occ_ids = lax.broadcasted_iota(jnp.int32, (per_dev, occ_count), 1)
    match_first = pair_list[:, 0][:, None] == occ_ids
    match_second = pair_list[:, 1][:, None] == occ_ids
    row_first = jnp.dot(match_first.astype(jnp.bfloat16), singles, preferred_element_type=jnp.float32)
    row_second = jnp.dot(match_second.astype(jnp.bfloat16), singles, preferred_element_type=jnp.float32)
    own_first = lax.dynamic_slice_in_dim(row_first, aux * rows_c, rows_c, 1)
    tau_own = (
        doubles.astype(jnp.float32) + own_first[:, :, None] * row_second[:, None, :]
    ).astype(jnp.bfloat16)

    dressing = singles[:, :win].T
    blank = jnp.zeros_like(dressing)
    lhs = jnp.concatenate(
        [jnp.concatenate([dressing, blank], axis=1), jnp.concatenate([blank, dressing], axis=1)], axis=0
    )
    rows = aux_count * win
    block = math.gcd(rows, 256)
    chunk = math.gcd(aux_count, 8)
    steps = aux_count // chunk
    sends = math.gcd(steps, 4)
    slots = min(3, steps)
    tile_rows = max(16, win)
    tile = doubles[:, :tile_rows, :128]

    dma = pltpu.SemaphoreType.DMA
    vmem = pl.BlockSpec(memory_space=pltpu.VMEM)
    anywhere = pl.BlockSpec(memory_space=pl.ANY)
    pieces, tiles = pl.pallas_call(
        functools.partial(ladder_kernel, n_pair, n_aux, group, win),
        out_shape=(
            jax.ShapeDtypeStruct((per_dev, win, block), jnp.float32),
            jax.ShapeDtypeStruct(tile.shape, tile.dtype),
        ),
        in_specs=[anywhere, vmem, vmem, vmem, anywhere],
        out_specs=(vmem, vmem),
        scratch_shapes=[
            pltpu.VMEM((lines, per_dev, width, width), jnp.bfloat16),
            pltpu.VMEM((group, rows, width), jnp.bfloat16),
            pltpu.VMEM((slots, chunk * occ_count, width), jnp.bfloat16),
            pltpu.VMEM((rows, width), jnp.bfloat16),
            pltpu.VMEM((lines * per_dev, block, block), jnp.float32),
            pltpu.VMEM((lines, per_dev, win, block), jnp.float32),
            pltpu.VMEM((lines, n_aux, per_dev, win, block), jnp.float32),
            pltpu.VMEM((n_aux,) + tile.shape, tile.dtype),
            dma, dma((slots,)),
            dma((2, lines, per_dev)), dma((lines, per_dev)),
            dma((lines, per_dev, n_aux)), dma((lines, per_dev, n_aux)),
            dma((cols, sends)), dma((cols, sends)),
            dma((cols, sends)), dma((cols, sends)),
            dma((lines, n_aux)), dma((lines, n_aux)),
            dma((n_aux,)), dma((n_aux,)),
        ],
        compiler_params=pltpu.CompilerParams(
            collective_id=0, has_side_effects=True, vmem_limit_bytes=50 * 1024 * 1024
        ),
        cost_estimate=pl.CostEstimate(
            flops=2 * lines * per_dev * group * rows * width * (width + block),
            bytes_accessed=2 * occ_slabs.size, transcendentals=0,
        ),
    )(tau_own, lhs, vir_slabs.reshape(rows, width), tile, occ_slabs.reshape(aux_count * occ_count, width))

    residual = jnp.sum(pieces.reshape(per_dev, win, block // win, win), axis=2)
    share_rows = win // n_aux
    row_start = aux * share_rows
    share = lax.dynamic_slice_in_dim(residual, row_start, share_rows, 1)
    own_doubles = lax.dynamic_slice_in_dim(tiles[:, :win, :win], row_start, share_rows, 1)
    own_vir = lax.dynamic_slice_in_dim(vir_energy, row_start, share_rows, 0)
    energy_first = jnp.sum(jnp.where(match_first, occ_energy[None, :], 0.0), axis=1)
    energy_second = jnp.sum(jnp.where(match_second, occ_energy[None, :], 0.0), axis=1)
    pair_energy = energy_first + energy_second
    denominator = pair_energy[:, None, None] - own_vir[None, :, None] - vir_energy[None, None, :]
    return own_doubles.astype(jnp.float32) + share / denominator


def solution(mesh):
    placed = (
        P("pair", "aux", None),
        P(),
        P(("aux", "pair"), None, None),
        P(("aux", "pair"), None, None),
        P(),
        P(),
        P("pair", None),
    )
    return jax.shard_map(
        functools.partial(body, mesh.shape["pair"], mesh.shape["aux"]),
        mesh=mesh, in_specs=placed, out_specs=P("pair", "aux", None), check_vma=False,
    )
```

```python
import functools
import math

import jax
import jax.numpy as jnp
from jax import lax
from jax.experimental import pallas as pl
from jax.experimental.pallas import tpu as pltpu
from jax.sharding import PartitionSpec as P

MESH = pl.DeviceIdType.MESH


def inner_group(n_pair):
    size = 2
    while size * size < n_pair:
        size *= 2
    return math.gcd(size, n_pair)


def ladder_kernel(
    n_pair, n_aux, group, win,
    pair_ref, energy_ref, doubles_ref, singles_ref, vir_hbm, occ_ref,
    out_ref, tile_out_ref, energy_out_ref,
    tau, dressed, slabs, total, fold, parts, tiles, own_ref, vir_ref, outer, lhs_ref,
    own_sem, vir_sem, slab_sem, z2_send, z2_recv, y2_send, y2_recv, z_send, z_recv, y_send, y_recv,
    x_send, x_recv, c_send, c_recv, r_send, r_recv, t_send, t_recv,
):
    lines = n_pair // group
    cols = group // 2
    per_dev, rows_c, width = doubles_ref.shape
    rows = vir_ref.shape[0]
    sends = x_recv.shape[1]
    send_rows = rows // sends
    slab_rows = slabs.shape[1]
    occ_count = singles_ref.shape[0]
    depth = lhs_ref.shape[1]
    tile_rows, tile_cols = tiles.shape[2:]
    extra = rows_c // 4 if n_aux > 1 and rows_c % 64 == 0 else 0
    steps = occ_ref.shape[0] // slab_rows
    step_rows = rows // steps
    block = total.shape[1]

    pair = lax.axis_index("pair")
    aux = lax.axis_index("aux")
    z = pair // group
    g = pair % group
    col = g // 2
    core = g % 2

    def at(zz, gg, aa):
        return {"pair": zz * group + gg, "aux": aa}

    def slab_copy(step):
        slot = lax.rem(step, slabs.shape[0])
        return pltpu.make_async_copy(
            occ_ref.at[pl.ds(step * slab_rows, slab_rows)], slabs.at[slot], slab_sem.at[slot]
        )

    depth_slots = slabs.shape[0]
    for step in range(min(depth_slots, steps)):
        slab_copy(step).start()
    own_rows = pl.ds(pl.multiple_of(aux * rows_c, rows_c), rows_c)
    own = pltpu.make_async_copy(doubles_ref, own_ref, own_sem)
    own.start()
    vir_copy = pltpu.make_async_copy(vir_hbm, vir_ref, vir_sem)
    vir_copy.start()

    barrier = pltpu.get_barrier_semaphore()
    for dz in range(lines):
        for da in range(n_aux):
            if dz or da:
                pl.semaphore_signal(
                    barrier, inc=1, device_id=at((z + dz) % lines, g, (aux + da) % n_aux), device_id_type=MESH
                )
    for dg in range(1, group):
        pl.semaphore_signal(barrier, inc=1, device_id=at(z, (g + dg) % group, aux), device_id_type=MESH)
    pl.semaphore_wait(barrier, lines * n_aux - 1 + group - 1)
    own.wait()

    pick = lax.broadcasted_iota(jnp.int32, (16, occ_count), 1)
    top = lax.broadcasted_iota(jnp.int32, (16, occ_count), 0) == 0

    def picked(index):
        one_hot = jnp.where(top & (pick == index), 1.0, 0.0).astype(jnp.bfloat16)
        return jnp.dot(one_hot, singles_ref[...], preferred_element_type=jnp.float32).astype(jnp.bfloat16)

    for k in range(per_dev):
        outer[...] = lax.dot_general(
            picked(pair_ref[k, 0]), picked(pair_ref[k, 1]), (((0,), (0,)), ((), ())),
            preferred_element_type=jnp.float32,
        )
        tau[z, k, own_rows] = (own_ref[k].astype(jnp.float32) + outer[own_rows, :]).astype(jnp.bfloat16)

    def piece(zz, k, aa):
        count = rows_c - extra if k == per_dev - 1 else rows_c
        return tau.at[zz, k, pl.ds(pl.multiple_of(aa * rows_c, rows_c), count)]

    def last_rows(zz, aa):
        start = pl.multiple_of(aa * rows_c + rows_c - extra, 16)
        return tau.at[zz, per_dev - 1, pl.ds(start, extra)]

    def z2_copy(zz, aa, way):
        ref = last_rows(zz, aa)
        return pltpu.make_async_remote_copy(
            src_ref=ref, dst_ref=ref, send_sem=z2_send.at[(way + 1) // 2, zz, aa],
            recv_sem=z2_recv.at[zz, aa], device_id=at(z + way, g, aux), device_id_type=MESH,
        )

    def y2_copy(aa, other):
        ref = last_rows(z, aa)
        return pltpu.make_async_remote_copy(
            src_ref=ref, dst_ref=ref, send_sem=y2_send.at[other],
            recv_sem=y2_recv.at[aa], device_id=at(z, g, other), device_id_type=MESH,
        )

    def onward2(zz, aa, ways):
        for way in ways:
            @pl.when((z + way >= 0) & (z + way < lines))
            def _():
                z2_copy(zz, aa, way).start()

    def spread2():
        for da in range(1, n_aux):
            source = (aux + da) % n_aux
            y2_copy(source, source).wait_recv()
            onward2(z, source, (-1, 1))

    def relay2(dist):
        for way in (-1, 1):
            source = z - way * dist

            @pl.when((source >= 0) & (source < lines))
            def _():
                for da in range(n_aux):
                    aa = (aux + da) % n_aux
                    z2_copy(source, aa, way).wait_recv()
                    onward2(source, aa, (way,))

    def z_copy(zz, k, way):
        ref = piece(zz, k, aux)
        return pltpu.make_async_remote_copy(
            src_ref=ref, dst_ref=ref, send_sem=z_send.at[(way + 1) // 2, zz, k],
            recv_sem=z_recv.at[zz, k], device_id=at(z + way, g, aux), device_id_type=MESH,
        )

    def y_copy(zz, k, aa, other):
        ref = piece(zz, k, aa)
        return pltpu.make_async_remote_copy(
            src_ref=ref, dst_ref=ref, send_sem=y_send.at[zz, k, other],
            recv_sem=y_recv.at[zz, k, aa], device_id=at(z, g, other), device_id_type=MESH,
        )

    def onward(zz, k, ways):
        for way in ways:
            @pl.when((z + way >= 0) & (z + way < lines))
            def _():
                z_copy(zz, k, way).start()
        for da in range(1, n_aux):
            y_copy(zz, k, aux, (aux + da) % n_aux).start()

    def relay(dist, k):
        for way in (-1, 1):
            source = z - way * dist

            @pl.when((source >= 0) & (source < lines))
            def _():
                z_copy(source, k, way).wait_recv()
                onward(source, k, (way,))

        if extra and k == per_dev - 1:
            relay2(dist)

    def x_copy(owner_col, part, to_col):
        ref = dressed.at[owner_col * 2 + core, pl.ds(part * send_rows, send_rows)]
        return pltpu.make_async_remote_copy(
            src_ref=ref, dst_ref=ref, send_sem=x_send.at[to_col, part],
            recv_sem=x_recv.at[owner_col, part], device_id=at(z, to_col * 2 + core, aux), device_id_type=MESH,
        )

    def c_copy(owner_col, owner_core, part):
        ref = dressed.at[owner_col * 2 + owner_core, pl.ds(part * send_rows, send_rows)]
        return pltpu.make_async_remote_copy(
            src_ref=ref, dst_ref=ref, send_sem=c_send.at[owner_col, part],
            recv_sem=c_recv.at[owner_col, part], device_id=at(z, col * 2 + 1 - core, aux), device_id_type=MESH,
        )

    def tile_copy(source, other):
        return pltpu.make_async_remote_copy(
            src_ref=tiles.at[source], dst_ref=tiles.at[source], send_sem=t_send.at[other],
            recv_sem=t_recv.at[source], device_id=at(z, g, other), device_id_type=MESH,
        )

    def other_cols():
        return [(col + dc) % cols for dc in range(1, cols)]

    def pass_block(part):
        for owner in other_cols():
            x_copy(owner, part, owner).wait_recv()
            c_copy(owner, core, part).start()

    if extra:
        for da in range(1, n_aux):
            y2_copy(aux, (aux + da) % n_aux).start()
    for k in range(per_dev):
        onward(z, k, (-1, 1))
    if extra:
        onward2(z, aux, (-1, 1))
    tiles[aux] = own_ref[:, :tile_rows, :tile_cols]
    for da in range(1, n_aux):
        tile_copy(aux, (aux + da) % n_aux).start()

    across = lax.broadcasted_iota(jnp.int32, (2 * win, width), 1)
    down = lax.broadcasted_iota(jnp.int32, (2 * win, width), 0)
    for half in range(2):
        chosen = (down // win == half) & (across == down - half * win)
        lhs_ref[:, half * occ_count:(half + 1) * occ_count] = lax.dot_general(
            jnp.where(chosen, 1.0, 0.0).astype(jnp.bfloat16), singles_ref[...],
            (((1,), (1,)), ((), ())), preferred_element_type=jnp.float32,
        ).astype(jnp.bfloat16)
    vir_copy.wait()

    def dress(step, carry):
        slab_copy(step).wait()
        slot = lax.rem(step, depth_slots)
        for i in range(slab_rows // depth):
            acc = jnp.dot(
                lhs_ref[...], slabs[slot, i * depth:(i + 1) * depth, :], preferred_element_type=jnp.float32
            )
            start = pl.multiple_of(step * step_rows + i * 2 * win, 2 * win)
            made = vir_ref[pl.ds(start, 2 * win), :].astype(jnp.float32) - acc
            dressed[g, pl.ds(start, 2 * win), :] = made.astype(jnp.bfloat16)

        @pl.when(step + depth_slots < steps)
        def _():
            slab_copy(step + depth_slots).start()
        return carry

    events = {}
    if extra:
        events.setdefault(min(steps, max(1, steps // 5)), []).append(spread2)
    if lines > 1:
        for k in range(per_dev):
            when = min(steps, max(1, (steps * (7 + 5 * k)) // 16))
            events.setdefault(when, []).append(functools.partial(relay, 1, k))
    passed = 0
    for part in range(sends):
        made_at = (part + 1) * steps // sends

        def send_own(part=part):
            for to_col in other_cols():
                x_copy(col, part, to_col).start()
            c_copy(col, core, part).start()

        events.setdefault(made_at, []).append(send_own)
        if part * 2 < sends:
            later = (part + 1) * steps // sends + (6 * steps) // 16
            if later < steps:
                events.setdefault(later, []).append(functools.partial(pass_block, part))
                passed = part + 1
    begin = 0
    for stop in sorted(events):
        if stop > begin:
            lax.fori_loop(begin, stop, dress, 0)
            begin = stop
        for action in events[stop]:
            action()
    if begin < steps:
        lax.fori_loop(begin, steps, dress, 0)

    total[...] = jnp.zeros_like(total)

    def unit(zz, k, gg):
        acc = None
        for i in range(rows // block):
            slab = dressed[gg, pl.ds(i * block, block), :]
            half = jnp.dot(slab, tau[zz, k], preferred_element_type=jnp.float32).astype(jnp.bfloat16)
            term = lax.dot_general(
                half, slab, (((1,), (1,)), ((), ())), preferred_element_type=jnp.float32
            )
            acc = term if acc is None else acc + term
        total[zz * per_dev + k] += acc

    def nth_group(i):
        return ((col + i // 2) % cols) * 2 + (core + i % 2) % 2

    def units(zz, k, first, last):
        def one(i, carry):
            unit(zz, k, nth_group(i))
            return carry

        lax.fori_loop(first, last, one, 0)

    def nth_line(t):
        near = jnp.minimum(z, lines - 1 - z)
        side = (t + 1) // 2 * (1 - 2 * (t % 2))
        rest = jnp.where(z + z <= lines - 1, t, lines - 1 - t)
        return jnp.where(t <= 2 * near, z + side, rest)

    def arrived(zz, k):
        for da in range(1, n_aux):
            source = (aux + da) % n_aux
            y_copy(zz, k, source, source).wait_recv()

    for k in range(per_dev):
        if lines > 2:
            relay(2, k)
        arrived(z, k)
        units(z, k, 0, 1)
        if k == 0:
            for part in range(sends):
                c_copy(col, 1 - core, part).wait_recv()
        units(z, k, 1, 2)
        for part in range(passed, min(sends, passed + 1)):
            pass_block(part)
            passed = part + 1
    for part in range(passed, sends):
        pass_block(part)
    for owner in other_cols():
        for part in range(sends):
            c_copy(owner, 1 - core, part).wait_recv()
    for k in range(per_dev):
        if lines > 3:
            relay(3, k)
        units(z, k, 2, group)
    for t in range(1, lines):
        zz = nth_line(t)
        for k in range(per_dev):
            if t + 3 < lines:
                relay(t + 3, k)
            arrived(zz, k)
            units(zz, k, 0, group)

    down = lax.broadcasted_iota(jnp.int32, (block, block), 0) // win
    across = lax.broadcasted_iota(jnp.int32, (block, block), 1) // win
    on_diagonal = down == across
    for zz in range(lines):
        for k in range(per_dev):
            kept = jnp.where(on_diagonal, total[zz * per_dev + k], 0.0)
            fold[zz, k] = jnp.sum(kept.reshape(block // win, win, block), axis=0)

    def sum_copy(source_z, source_aux, to_z, to_aux):
        return pltpu.make_async_remote_copy(
            src_ref=fold.at[to_z], dst_ref=parts.at[source_z, source_aux],
            send_sem=r_send.at[to_z, to_aux], recv_sem=r_recv.at[source_z, source_aux],
            device_id=at(to_z, g, to_aux), device_id_type=MESH,
        )

    others = [
        ((z + dz) % lines, (aux + da) % n_aux)
        for dz in range(lines) for da in range(n_aux) if dz or da
    ]
    for to_z, to_aux in others:
        sum_copy(z, aux, to_z, to_aux).start()
    parts[z, aux] = fold[z]
    for from_z, from_aux in others:
        sum_copy(from_z, from_aux, from_z, from_aux).wait_recv()
    result = parts[0, 0]
    for i in range(1, lines * n_aux):
        result = result + parts[i // n_aux, i % n_aux]
    out_ref[...] = result
    for da in range(1, n_aux):
        source = (aux + da) % n_aux
        tile_copy(source, source).wait_recv()
    tile_out_ref[...] = tiles[0]
    for k in range(per_dev):
        energy_out_ref[k] = jnp.full(
            energy_out_ref.shape[1:], energy_ref[pair_ref[k, 0]] + energy_ref[pair_ref[k, 1]], jnp.float32
        )

    for to_z, to_aux in others:
        sum_copy(z, aux, to_z, to_aux).wait_send()
    for da in range(1, n_aux):
        tile_copy(aux, (aux + da) % n_aux).wait_send()
    for part in range(sends):
        for to_col in other_cols():
            x_copy(col, part, to_col).wait_send()
        for dc in range(cols):
            c_copy((col + dc) % cols, core, part).wait_send()
    if extra:
        for da in range(1, n_aux):
            y2_copy(aux, (aux + da) % n_aux).wait_send()
        for zz in range(lines):
            @pl.when((zz <= z) & (z + 1 < lines))
            def _():
                for aa in range(n_aux):
                    z2_copy(zz, aa, 1).wait_send()

            @pl.when((zz >= z) & (z >= 1))
            def _():
                for aa in range(n_aux):
                    z2_copy(zz, aa, -1).wait_send()
    for k in range(per_dev):
        for zz in range(lines):
            for da in range(1, n_aux):
                y_copy(zz, k, aux, (aux + da) % n_aux).wait_send()

            @pl.when((zz <= z) & (z + 1 < lines))
            def _():
                z_copy(zz, k, 1).wait_send()

            @pl.when((zz >= z) & (z >= 1))
            def _():
                z_copy(zz, k, -1).wait_send()


def body(n_pair, n_aux, doubles, singles, vir_slabs, occ_slabs, occ_energy, vir_energy, pair_list):
    per_dev, rows_c, width = doubles.shape
    aux_count, win, _ = vir_slabs.shape
    occ_count = singles.shape[0]
    group = inner_group(n_pair)
    lines = n_pair // group
    cols = group // 2
    aux = lax.axis_index("aux")

    rows = aux_count * win
    block = math.gcd(rows, 256)
    chunk = math.gcd(aux_count, 8)
    steps = aux_count // chunk
    sends = math.gcd(steps, 4)
    slots = min(6, steps)
    tile_rows = max(16, win)
    tile_shape = (per_dev, tile_rows, min(width, 128))

    dma = pltpu.SemaphoreType.DMA
    vmem = pl.BlockSpec(memory_space=pltpu.VMEM)
    smem = pl.BlockSpec(memory_space=pltpu.SMEM)
    anywhere = pl.BlockSpec(memory_space=pl.ANY)
    pieces, tiles, energies = pl.pallas_call(
        functools.partial(ladder_kernel, n_pair, n_aux, group, win),
        out_shape=(
            jax.ShapeDtypeStruct((per_dev, win, block), jnp.float32),
            jax.ShapeDtypeStruct(tile_shape, doubles.dtype),
            jax.ShapeDtypeStruct((per_dev, 8, 128), jnp.float32),
        ),
        in_specs=[smem, smem, anywhere, vmem, anywhere, anywhere],
        out_specs=(vmem, vmem, vmem),
        scratch_shapes=[
            pltpu.VMEM((lines, per_dev, width, width), jnp.bfloat16),
            pltpu.VMEM((group, rows, width), jnp.bfloat16),
            pltpu.VMEM((slots, chunk * occ_count, width), jnp.bfloat16),
            pltpu.VMEM((lines * per_dev, block, block), jnp.float32),
            pltpu.VMEM((lines, per_dev, win, block), jnp.float32),
            pltpu.VMEM((lines, n_aux, per_dev, win, block), jnp.float32),
            pltpu.VMEM((n_aux,) + tile_shape, doubles.dtype),
            pltpu.VMEM(doubles.shape, doubles.dtype),
            pltpu.VMEM((rows, width), jnp.bfloat16),
            pltpu.VMEM((width, width), jnp.float32),
            pltpu.VMEM((2 * win, 2 * occ_count), jnp.bfloat16),
            dma, dma, dma((slots,)),
            dma((2, lines, n_aux)), dma((lines, n_aux)), dma((n_aux,)), dma((n_aux,)),
            dma((2, lines, per_dev)), dma((lines, per_dev)),
            dma((lines, per_dev, n_aux)), dma((lines, per_dev, n_aux)),
            dma((cols, sends)), dma((cols, sends)),
            dma((cols, sends)), dma((cols, sends)),
            dma((lines, n_aux)), dma((lines, n_aux)),
            dma((n_aux,)), dma((n_aux,)),
        ],
        compiler_params=pltpu.CompilerParams(
            collective_id=0, has_side_effects=True, vmem_limit_bytes=56 * 1024 * 1024
        ),
        cost_estimate=pl.CostEstimate(
            flops=2 * lines * per_dev * group * rows * width * (width + block),
            bytes_accessed=2 * occ_slabs.size, transcendentals=0,
        ),
    )(
        pair_list, occ_energy, doubles, singles, vir_slabs.reshape(rows, width),
        occ_slabs.reshape(aux_count * occ_count, width),
    )

    residual = jnp.sum(pieces.reshape(per_dev, win, block // win, win), axis=2)
    share_rows = win // n_aux
    row_start = aux * share_rows
    share = lax.dynamic_slice_in_dim(residual, row_start, share_rows, 1)
    own_doubles = lax.dynamic_slice_in_dim(tiles[:, :win, :win], row_start, share_rows, 1)
    own_vir = lax.dynamic_slice_in_dim(vir_energy, row_start, share_rows, 0)
    pair_energy = energies[:, 0, 0]
    denominator = pair_energy[:, None, None] - own_vir[None, :, None] - vir_energy[None, None, :]
    return own_doubles.astype(jnp.float32) + share / denominator


def solution(mesh):
    placed = (
        P("pair", "aux", None),
        P(),
        P(("aux", "pair"), None, None),
        P(("aux", "pair"), None, None),
        P(),
        P(),
        P("pair", None),
    )
    return jax.shard_map(
        functools.partial(body, mesh.shape["pair"], mesh.shape["aux"]),
        mesh=mesh, in_specs=placed, out_specs=P("pair", "aux", None), check_vma=False,
    )
```

```python
import functools
import math

import jax
import jax.numpy as jnp
from jax import lax
from jax.experimental import pallas as pl
from jax.experimental.pallas import tpu as pltpu
from jax.sharding import PartitionSpec as P

MESH = pl.DeviceIdType.MESH


def inner_group(n_pair):
    size = 2
    while size * size < n_pair:
        size *= 2
    return math.gcd(size, n_pair)


def ladder_kernel(
    n_pair, n_aux, group, win,
    pair_ref, energy_ref, doubles_ref, singles_ref, vir_hbm, occ_ref,
    out_ref, tile_out_ref, energy_out_ref,
    tau, dressed, slabs, total, fold, parts, tiles, own_ref, vir_ref, outer, lhs_ref,
    own_sem, vir_sem, slab_sem, z_send, z_recv, y_send, y_recv,
    x_send, x_recv, c_send, c_recv, r_send, r_recv, t_send, t_recv,
):
    lines = n_pair // group
    cols = group // 2
    per_dev, rows_c, width = doubles_ref.shape
    rows = vir_ref.shape[0]
    sends = x_recv.shape[1]
    send_rows = rows // sends
    slab_rows = slabs.shape[1]
    occ_count = singles_ref.shape[0]
    depth = lhs_ref.shape[1]
    tile_rows, tile_cols = tiles.shape[2:]
    steps = occ_ref.shape[0] // slab_rows
    step_rows = rows // steps
    block = total.shape[1]

    pair = lax.axis_index("pair")
    aux = lax.axis_index("aux")
    z = pair // group
    g = pair % group
    col = g // 2
    core = g % 2

    def at(zz, gg, aa):
        return {"pair": zz * group + gg, "aux": aa}

    def slab_copy(step):
        slot = lax.rem(step, slabs.shape[0])
        return pltpu.make_async_copy(
            occ_ref.at[pl.ds(step * slab_rows, slab_rows)], slabs.at[slot], slab_sem.at[slot]
        )

    depth_slots = slabs.shape[0]
    for step in range(min(depth_slots, steps)):
        slab_copy(step).start()
    own_rows = pl.ds(pl.multiple_of(aux * rows_c, rows_c), rows_c)
    own = pltpu.make_async_copy(doubles_ref, own_ref, own_sem)
    own.start()
    vir_copy = pltpu.make_async_copy(vir_hbm, vir_ref, vir_sem)
    vir_copy.start()

    barrier = pltpu.get_barrier_semaphore()
    for dz in range(lines):
        for da in range(n_aux):
            if dz or da:
                pl.semaphore_signal(
                    barrier, inc=1, device_id=at((z + dz) % lines, g, (aux + da) % n_aux), device_id_type=MESH
                )
    for dg in range(1, group):
        pl.semaphore_signal(barrier, inc=1, device_id=at(z, (g + dg) % group, aux), device_id_type=MESH)
    pl.semaphore_wait(barrier, lines * n_aux - 1 + group - 1)
    own.wait()

    pick = lax.broadcasted_iota(jnp.int32, (16, occ_count), 1)
    top = lax.broadcasted_iota(jnp.int32, (16, occ_count), 0) == 0

    def picked(index):
        one_hot = jnp.where(top & (pick == index), 1.0, 0.0).astype(jnp.bfloat16)
        return jnp.dot(one_hot, singles_ref[...], preferred_element_type=jnp.float32).astype(jnp.bfloat16)

    for k in range(per_dev):
        outer[...] = lax.dot_general(
            picked(pair_ref[k, 0]), picked(pair_ref[k, 1]), (((0,), (0,)), ((), ())),
            preferred_element_type=jnp.float32,
        )
        tau[z, k, own_rows] = (own_ref[k].astype(jnp.float32) + outer[own_rows, :]).astype(jnp.bfloat16)

    def piece(zz, k, aa):
        return tau.at[zz, k, pl.ds(pl.multiple_of(aa * rows_c, rows_c), rows_c)]

    def z_copy(zz, k, way):
        ref = piece(zz, k, aux)
        return pltpu.make_async_remote_copy(
            src_ref=ref, dst_ref=ref, send_sem=z_send.at[(way + 1) // 2, zz, k],
            recv_sem=z_recv.at[zz, k], device_id=at(z + way, g, aux), device_id_type=MESH,
        )

    def y_copy(zz, k, aa, other):
        ref = piece(zz, k, aa)
        return pltpu.make_async_remote_copy(
            src_ref=ref, dst_ref=ref, send_sem=y_send.at[zz, k, other],
            recv_sem=y_recv.at[zz, k, aa], device_id=at(z, g, other), device_id_type=MESH,
        )

    def onward(zz, k, ways):
        for way in ways:
            @pl.when((z + way >= 0) & (z + way < lines))
            def _():
                z_copy(zz, k, way).start()
        for da in range(1, n_aux):
            y_copy(zz, k, aux, (aux + da) % n_aux).start()

    def relay(dist, k):
        for way in (-1, 1):
            source = z - way * dist

            @pl.when((source >= 0) & (source < lines))
            def _():
                z_copy(source, k, way).wait_recv()
                onward(source, k, (way,))

    def x_copy(owner_col, part, to_col):
        ref = dressed.at[owner_col * 2 + core, pl.ds(part * send_rows, send_rows)]
        return pltpu.make_async_remote_copy(
            src_ref=ref, dst_ref=ref, send_sem=x_send.at[to_col, part],
            recv_sem=x_recv.at[owner_col, part], device_id=at(z, to_col * 2 + core, aux), device_id_type=MESH,
        )

    def c_copy(owner_col, owner_core, part):
        ref = dressed.at[owner_col * 2 + owner_core, pl.ds(part * send_rows, send_rows)]
        return pltpu.make_async_remote_copy(
            src_ref=ref, dst_ref=ref, send_sem=c_send.at[owner_col, part],
            recv_sem=c_recv.at[owner_col, part], device_id=at(z, col * 2 + 1 - core, aux), device_id_type=MESH,
        )

    def tile_copy(source, other):
        return pltpu.make_async_remote_copy(
            src_ref=tiles.at[source], dst_ref=tiles.at[source], send_sem=t_send.at[other],
            recv_sem=t_recv.at[source], device_id=at(z, g, other), device_id_type=MESH,
        )

    def other_cols():
        return [(col + dc) % cols for dc in range(1, cols)]

    def pass_block(part):
        for owner in other_cols():
            x_copy(owner, part, owner).wait_recv()
            c_copy(owner, core, part).start()

    for k in range(per_dev):
        onward(z, k, (-1, 1))
    tiles[aux] = own_ref[:, :tile_rows, :tile_cols]
    for da in range(1, n_aux):
        tile_copy(aux, (aux + da) % n_aux).start()

    across = lax.broadcasted_iota(jnp.int32, (2 * win, width), 1)
    down = lax.broadcasted_iota(jnp.int32, (2 * win, width), 0)
    for half in range(2):
        chosen = (down // win == half) & (across == down - half * win)
        lhs_ref[:, half * occ_count:(half + 1) * occ_count] = lax.dot_general(
            jnp.where(chosen, 1.0, 0.0).astype(jnp.bfloat16), singles_ref[...],
            (((1,), (1,)), ((), ())), preferred_element_type=jnp.float32,
        ).astype(jnp.bfloat16)
    vir_copy.wait()

    def dress(step, carry):
        slab_copy(step).wait()
        slot = lax.rem(step, depth_slots)
        for i in range(slab_rows // depth):
            acc = jnp.dot(
                lhs_ref[...], slabs[slot, i * depth:(i + 1) * depth, :], preferred_element_type=jnp.float32
            )
            start = pl.multiple_of(step * step_rows + i * 2 * win, 2 * win)
            made = vir_ref[pl.ds(start, 2 * win), :].astype(jnp.float32) - acc
            dressed[g, pl.ds(start, 2 * win), :] = made.astype(jnp.bfloat16)

        @pl.when(step + depth_slots < steps)
        def _():
            slab_copy(step + depth_slots).start()
        return carry

    events = {}
    if lines > 1:
        for k in range(per_dev):
            when = min(steps, max(1, (steps * (9 + 7 * k)) // 16))
            events.setdefault(when, []).append(functools.partial(relay, 1, k))
    passed = 0
    for part in range(sends):
        made_at = (part + 1) * steps // sends

        def send_own(part=part):
            for to_col in other_cols():
                x_copy(col, part, to_col).start()
            c_copy(col, core, part).start()

        events.setdefault(made_at, []).append(send_own)
        if part * 2 < sends:
            later = (part + 1) * steps // sends + steps // 2
            if later < steps:
                events.setdefault(later, []).append(functools.partial(pass_block, part))
                passed = part + 1
    begin = 0
    for stop in sorted(events):
        if stop > begin:
            lax.fori_loop(begin, stop, dress, 0)
            begin = stop
        for action in events[stop]:
            action()
    if begin < steps:
        lax.fori_loop(begin, steps, dress, 0)

    total[...] = jnp.zeros_like(total)

    def unit(zz, k, gg):
        acc = None
        for i in range(rows // block):
            slab = dressed[gg, pl.ds(i * block, block), :]
            half = jnp.dot(slab, tau[zz, k], preferred_element_type=jnp.float32).astype(jnp.bfloat16)
            term = lax.dot_general(
                half, slab, (((1,), (1,)), ((), ())), preferred_element_type=jnp.float32
            )
            acc = term if acc is None else acc + term
        total[zz * per_dev + k] += acc

    def nth_group(i):
        return ((col + i // 2) % cols) * 2 + (core + i % 2) % 2

    def units(zz, k, first, last):
        def one(i, carry):
            unit(zz, k, nth_group(i))
            return carry

        lax.fori_loop(first, last, one, 0)

    def nth_line(t):
        near = jnp.minimum(z, lines - 1 - z)
        side = (t + 1) // 2 * (1 - 2 * (t % 2))
        rest = jnp.where(z + z <= lines - 1, t, lines - 1 - t)
        return jnp.where(t <= 2 * near, z + side, rest)

    def arrived(zz, k):
        for da in range(1, n_aux):
            source = (aux + da) % n_aux
            y_copy(zz, k, source, source).wait_recv()

    for k in range(per_dev):
        arrived(z, k)
        units(z, k, 0, 1)
        if k == 0:
            for part in range(sends):
                c_copy(col, 1 - core, part).wait_recv()
        units(z, k, 1, 2)
        if k == 0 and passed < sends:
            pass_block(passed)
            passed += 1
    for k in range(per_dev):
        if lines > 2:
            relay(2, k)
        if passed < sends:
            pass_block(passed)
            passed += 1
        if lines > 1:
            arrived(nth_line(1), k)
            units(nth_line(1), k, 0, 2)
    for part in range(passed, sends):
        pass_block(part)
    for owner in other_cols():
        for part in range(sends):
            c_copy(owner, 1 - core, part).wait_recv()
    for k in range(per_dev):
        units(z, k, 2, group)
    for k in range(per_dev):
        if lines > 3:
            relay(3, k)
        if lines > 1:
            units(nth_line(1), k, 2, group)
    for t in range(2, lines):
        zz = nth_line(t)
        for k in range(per_dev):
            if t + 2 < lines:
                relay(t + 2, k)
            arrived(zz, k)
            units(zz, k, 0, group)

    down = lax.broadcasted_iota(jnp.int32, (block, block), 0) // win
    across = lax.broadcasted_iota(jnp.int32, (block, block), 1) // win
    on_diagonal = down == across
    for zz in range(lines):
        for k in range(per_dev):
            kept = jnp.where(on_diagonal, total[zz * per_dev + k], 0.0)
            fold[zz, k] = jnp.sum(kept.reshape(block // win, win, block), axis=0)

    def sum_copy(source_z, source_aux, to_z, to_aux):
        return pltpu.make_async_remote_copy(
            src_ref=fold.at[to_z], dst_ref=parts.at[source_z, source_aux],
            send_sem=r_send.at[to_z, to_aux], recv_sem=r_recv.at[source_z, source_aux],
            device_id=at(to_z, g, to_aux), device_id_type=MESH,
        )

    others = [
        ((z + dz) % lines, (aux + da) % n_aux)
        for dz in range(lines) for da in range(n_aux) if dz or da
    ]
    for to_z, to_aux in others:
        sum_copy(z, aux, to_z, to_aux).start()
    parts[z, aux] = fold[z]
    for from_z, from_aux in others:
        sum_copy(from_z, from_aux, from_z, from_aux).wait_recv()
    result = parts[0, 0]
    for i in range(1, lines * n_aux):
        result = result + parts[i // n_aux, i % n_aux]
    out_ref[...] = result
    for da in range(1, n_aux):
        source = (aux + da) % n_aux
        tile_copy(source, source).wait_recv()
    tile_out_ref[...] = tiles[0]
    for k in range(per_dev):
        energy_out_ref[k] = jnp.full(
            energy_out_ref.shape[1:], energy_ref[pair_ref[k, 0]] + energy_ref[pair_ref[k, 1]], jnp.float32
        )

    for to_z, to_aux in others:
        sum_copy(z, aux, to_z, to_aux).wait_send()
    for da in range(1, n_aux):
        tile_copy(aux, (aux + da) % n_aux).wait_send()
    for part in range(sends):
        for to_col in other_cols():
            x_copy(col, part, to_col).wait_send()
        for dc in range(cols):
            c_copy((col + dc) % cols, core, part).wait_send()
    for k in range(per_dev):
        for zz in range(lines):
            for da in range(1, n_aux):
                y_copy(zz, k, aux, (aux + da) % n_aux).wait_send()

            @pl.when((zz <= z) & (z + 1 < lines))
            def _():
                z_copy(zz, k, 1).wait_send()

            @pl.when((zz >= z) & (z >= 1))
            def _():
                z_copy(zz, k, -1).wait_send()


def body(n_pair, n_aux, doubles, singles, vir_slabs, occ_slabs, occ_energy, vir_energy, pair_list):
    per_dev, rows_c, width = doubles.shape
    aux_count, win, _ = vir_slabs.shape
    occ_count = singles.shape[0]
    group = inner_group(n_pair)
    lines = n_pair // group
    cols = group // 2
    aux = lax.axis_index("aux")

    rows = aux_count * win
    block = math.gcd(rows, 256)
    chunk = math.gcd(aux_count, 8)
    steps = aux_count // chunk
    sends = math.gcd(steps, 4)
    slots = min(6, steps)
    tile_rows = max(16, win)
    tile_shape = (per_dev, tile_rows, min(width, 128))

    dma = pltpu.SemaphoreType.DMA
    vmem = pl.BlockSpec(memory_space=pltpu.VMEM)
    smem = pl.BlockSpec(memory_space=pltpu.SMEM)
    anywhere = pl.BlockSpec(memory_space=pl.ANY)
    pieces, tiles, energies = pl.pallas_call(
        functools.partial(ladder_kernel, n_pair, n_aux, group, win),
        out_shape=(
            jax.ShapeDtypeStruct((per_dev, win, block), jnp.float32),
            jax.ShapeDtypeStruct(tile_shape, doubles.dtype),
            jax.ShapeDtypeStruct((per_dev, win // n_aux, win), jnp.float32),
        ),
        in_specs=[smem, smem, anywhere, vmem, anywhere, anywhere],
        out_specs=(vmem, vmem, vmem),
        scratch_shapes=[
            pltpu.VMEM((lines, per_dev, width, width), jnp.bfloat16),
            pltpu.VMEM((group, rows, width), jnp.bfloat16),
            pltpu.VMEM((slots, chunk * occ_count, width), jnp.bfloat16),
            pltpu.VMEM((lines * per_dev, block, block), jnp.float32),
            pltpu.VMEM((lines, per_dev, win, block), jnp.float32),
            pltpu.VMEM((lines, n_aux, per_dev, win, block), jnp.float32),
            pltpu.VMEM((n_aux,) + tile_shape, doubles.dtype),
            pltpu.VMEM(doubles.shape, doubles.dtype),
            pltpu.VMEM((rows, width), jnp.bfloat16),
            pltpu.VMEM((width, width), jnp.float32),
            pltpu.VMEM((2 * win, 2 * occ_count), jnp.bfloat16),
            dma, dma, dma((slots,)),
            dma((2, lines, per_dev)), dma((lines, per_dev)),
            dma((lines, per_dev, n_aux)), dma((lines, per_dev, n_aux)),
            dma((cols, sends)), dma((cols, sends)),
            dma((cols, sends)), dma((cols, sends)),
            dma((lines, n_aux)), dma((lines, n_aux)),
            dma((n_aux,)), dma((n_aux,)),
        ],
        compiler_params=pltpu.CompilerParams(
            collective_id=0, has_side_effects=True, vmem_limit_bytes=56 * 1024 * 1024
        ),
        cost_estimate=pl.CostEstimate(
            flops=2 * lines * per_dev * group * rows * width * (width + block),
            bytes_accessed=2 * occ_slabs.size, transcendentals=0,
        ),
    )(
        pair_list, occ_energy, doubles, singles, vir_slabs.reshape(rows, width),
        occ_slabs.reshape(aux_count * occ_count, width),
    )

    residual = jnp.sum(pieces.reshape(per_dev, win, block // win, win), axis=2)
    share_rows = win // n_aux
    row_start = aux * share_rows
    share = lax.dynamic_slice_in_dim(residual, row_start, share_rows, 1)
    own_doubles = lax.dynamic_slice_in_dim(tiles[:, :win, :win], row_start, share_rows, 1)
    own_vir = lax.dynamic_slice_in_dim(vir_energy, row_start, share_rows, 0)
    denominator = energies - own_vir[None, :, None] - vir_energy[None, None, :]
    return own_doubles.astype(jnp.float32) + share / denominator


def solution(mesh):
    placed = (
        P("pair", "aux", None),
        P(),
        P(("aux", "pair"), None, None),
        P(("aux", "pair"), None, None),
        P(),
        P(),
        P("pair", None),
    )
    return jax.shard_map(
        functools.partial(body, mesh.shape["pair"], mesh.shape["aux"]),
        mesh=mesh, in_specs=placed, out_specs=P("pair", "aux", None), check_vma=False,
    )
```
